512 devices in a mesh: rep: 32 (over z, x_lo), fsdp: 16 (over y, x_hi, core).
Axes of the slice: x: 4 (x_hi: 2, x_lo: 2; x = x_hi * 2 + x_lo), y: 4, z: 16, core: 2. Of those that a mesh axis runs over, the one named last changes fastest.
Arguments:
- activations: bfloat16 [32, 3072, 4096], P('rep', 'fsdp'), may hold values from -6 to 6
- weights: float32 [32, 4096, 512], P('rep', 'fsdp'), may hold values from -6 to 6
- cotangent: bfloat16 [32, 3072, 512], P('rep', 'fsdp'), may hold values from -6 to 6
- step_index: int32 [1], replicated, may hold values from 0 to 999
Outputs:
- projected: bfloat16 [32, 3072, 512], P('rep', 'fsdp')
- input_grad: bfloat16 [32, 3072, 4096], P('rep', 'fsdp')
- mixed: float32 [32, 4096, 512], P('rep', 'fsdp')
The draws below stay inside these ranges and needn't reach their ends.
All inputs are finite; a program needn't handle non-finite values.
Results may differ from the reference program's by a relative error of at most 0.005.
Values may be sent and summed in bfloat16 or wider, within the bound.
No kernel may reach another device: no remote copies, remote signals or barrier semaphores. Data moves between devices by JAX's collectives and lax.ppermute only.
A program may use at most 64 MiB of HBM per device.

```python
import jax
import jax.numpy as jnp
from jax import lax

D = 4096
KW = 512
TOK_DEV = 192
TOKENS = 3072
REPLICAS = 32
BITS = 3
N_FSDP = 16


def spiked(drawn, key, source, target, parts, factor):
    def block_of(position):
        return (jnp.arange(drawn.shape[position]) // (drawn.shape[position] // parts)).reshape((-1,) + (1,) * (drawn.ndim - 1 - position))

    near = jax.random.permutation(key, parts)[block_of(target)]
    far = (block_of(target) + parts // 2) % parts
    return jnp.where((block_of(source) == near) | (block_of(source) == far), factor * drawn, drawn)


def shard_levels(rng, dims, split, low, high):
    level, own = 1.0, jax.random.fold_in(rng, 6)
    for axis_at, blocks in split:
        steps = jnp.exp(jax.random.uniform(jax.random.fold_in(own, axis_at), (blocks,), jnp.float32, low / len(split), high / len(split)))
        level = level * jnp.repeat(steps, dims[axis_at] // blocks).reshape([-1 if axis == axis_at else 1 for axis in range(len(dims))])
    return level


def centred(rng, dims, width, most, shards=(), kind=jnp.bfloat16):
    array = jax.random.normal(rng, dims, jnp.float32) * width
    if len(shards) > 0:
        array = shard_levels(rng, dims, shards, -0.22, 0.18) * array
    return jnp.clip(array, min=-most, max=most).astype(kind)


def noise_with(key, shape, scale, limit, pieces, heavy, held_as=jnp.bfloat16):
    array = scale * jax.random.normal(key, shape, jnp.float32)
    if pieces:
        array = array * shard_levels(key, shape, pieces, -0.22, 0.18)
    return jnp.clip(spiked(array, jax.random.fold_in(key, 3), *heavy), -limit, limit).astype(held_as)


def setup_inputs(seed: int = 0) -> dict:
    splits = jax.random.split(jax.random.key(seed), 5)
    return {
        "activations": noise_with(splits[0], (REPLICAS, TOKENS, D), 1.0, 6.0, ((0, 32), (1, 16)), (1, 2, 16, 2.0)),
        "weights": centred(splits[1], (REPLICAS, D, KW), 1.0, 6.0, ((0, 32), (1, 16)), jnp.float32),
        "cotangent": centred(splits[2], (REPLICAS, TOKENS, KW), 1.0, 6.0, ((0, 32), (1, 16))),
        "step_index": jax.random.randint(splits[3], (1,), 0, 1000).astype(jnp.int32),
    }


def one_replica(items):
    inputs, master, cotan, rate = items
    scale = D ** (-0.5)
    half_weights = master.astype(jnp.bfloat16)
    projected = (jnp.dot(inputs, half_weights, preferred_element_type=jnp.float32) * scale).astype(jnp.bfloat16)
    back = jnp.dot(cotan, half_weights.T, preferred_element_type=jnp.float32)
    input_grad = (back * scale).astype(jnp.bfloat16)
    blocks_in = inputs.reshape(N_FSDP, TOK_DEV, D).astype(jnp.float32)
    blocks_co = cotan.reshape(N_FSDP, TOK_DEV, KW).astype(jnp.float32)
    partial_terms = (jnp.einsum('btd,btk->bdk', blocks_in, blocks_co) * scale).astype(jnp.bfloat16)
    partial_terms = lax.optimization_barrier(partial_terms)
    grad = lax.optimization_barrier(jnp.sum(partial_terms.astype(jnp.float32), axis=0))
    updated = master - rate * grad
    return (projected, input_grad, updated)

def reference(activations, weights, cotangent, step_index):
    rate = 0.3 / jnp.sqrt(1.0 + step_index[0].astype(jnp.float32) / 50.0)
    rates = jnp.full((REPLICAS,), rate, dtype=jnp.float32)
    projected, input_grad, updated = lax.map(one_replica, (activations, weights, cotangent, rates))
    bit = step_index[0] % BITS
    partners = jnp.arange(REPLICAS, dtype=jnp.int32) ^ jnp.left_shift(jnp.int32(1), bit)
    mixed = 0.5 * (updated + jnp.take(updated, partners, axis=0))
    return (projected, input_grad, mixed)
```

```python
from functools import partial

import jax
import jax.numpy as jnp
from jax import lax
from jax.experimental import pallas as pl
from jax.experimental.pallas import tpu as pltpu
from jax.sharding import PartitionSpec as P

D = 4096
KW = 512
BITS = 3
CORES = 2
SPAN = 2
RINGS = 4
SIDES = CORES * SPAN
ROWS = D // (SIDES * RINGS)
SCALE = D ** (-0.5)
ALONG_Y = [[side + SIDES * y for y in range(RINGS)] for side in range(SIDES)]
IN_VMEM = pl.BlockSpec(memory_space=pltpu.VMEM)
IN_SMEM = pl.BlockSpec(memory_space=pltpu.SMEM)
PARAMS = pltpu.CompilerParams(vmem_limit_bytes=16 << 20)


def swapped(block, axis, apart):
    count = lax.axis_size(axis)
    return lax.ppermute(block, axis, [(low, low ^ apart) for low in range(count)])


def along_y(block):
    return lax.all_to_all(block, "fsdp", 0, 0, tiled=True, axis_index_groups=ALONG_Y)


def shifted(block, hops):
    count = SIDES * RINGS
    return lax.ppermute(block, "fsdp", [(place, (place + SIDES * hops) % count) for place in range(count)])


def after(value, earlier):
    return lax.optimization_barrier((value, earlier))[0]


def columns(block):
    return pl.ds(pl.multiple_of(block * ROWS, ROWS), ROWS)


def terms_kernel(spot, inputs, partner_inputs, cotan, partner_cotan, kept, given):
    turned = cotan[...].T
    partner_turned = partner_cotan[...].T
    for out, side in ((kept, spot[1]), (given, 1 - spot[1])):
        for y in range(RINGS):
            at = columns(SIDES * y + CORES * side + spot[0])
            total = jnp.dot(turned, inputs[:, at], preferred_element_type=jnp.float32)
            total += jnp.dot(partner_turned, partner_inputs[:, at], preferred_element_type=jnp.float32)
            out[y] = (total * SCALE).astype(jnp.bfloat16)


def terms_of(spot, inputs, partner_inputs, cotan, partner_cotan):
    return pl.pallas_call(
        terms_kernel,
        in_specs=[IN_SMEM] + [IN_VMEM] * 4,
        out_specs=[IN_VMEM] * 2,
        out_shape=[jax.ShapeDtypeStruct((RINGS, KW, ROWS), jnp.bfloat16)] * 2,
        compiler_params=PARAMS,
        cost_estimate=pl.CostEstimate(flops=inputs.size, bytes_accessed=1 << 20, transcendentals=0),
        name="gradient_terms",
    )(spot, inputs, partner_inputs, cotan, partner_cotan)


def copies_kernel(master, near, out):
    for y in range(RINGS):
        out[y, 0] = master[...].astype(jnp.bfloat16)
        out[y, 1] = near[...]


def copies_of(master, near):
    return pl.pallas_call(
        copies_kernel,
        in_specs=[IN_VMEM] * 2,
        out_specs=IN_VMEM,
        out_shape=jax.ShapeDtypeStruct((RINGS, SPAN, ROWS, KW), jnp.bfloat16),
        compiler_params=PARAMS,
        cost_estimate=pl.CostEstimate(flops=1 << 38, bytes_accessed=3 << 20, transcendentals=0),
        name="copies",
    )(master, near)


def fold_kernel(spot, kept, taken, *sent):
    for hops, out in zip((1, 2, 3), sent):
        y = lax.rem(spot[2] + hops, RINGS)
        out[...] = (kept[y].astype(jnp.float32) + taken[y].astype(jnp.float32)).astype(jnp.bfloat16)


def fold_of(spot, kept, taken):
    return pl.pallas_call(
        fold_kernel,
        in_specs=[IN_SMEM] + [IN_VMEM] * 2,
        out_specs=[IN_VMEM] * (RINGS - 1),
        out_shape=[jax.ShapeDtypeStruct((KW, ROWS), jnp.bfloat16)] * (RINGS - 1),
        compiler_params=PARAMS,
        cost_estimate=pl.CostEstimate(flops=1 << 38, bytes_accessed=3 << 20, transcendentals=0),
        name="fold",
    )(spot, kept, taken)


def own_kernel(spot, kept, taken, own):
    own[...] = kept[spot[2]].astype(jnp.float32) + taken[spot[2]].astype(jnp.float32)


def own_of(spot, kept, taken):
    return pl.pallas_call(
        own_kernel,
        in_specs=[IN_SMEM] + [IN_VMEM] * 2,
        out_specs=IN_VMEM,
        out_shape=jax.ShapeDtypeStruct((KW, ROWS), jnp.float32),
        compiler_params=PARAMS,
        cost_estimate=pl.CostEstimate(flops=1 << 38, bytes_accessed=3 << 20, transcendentals=0),
        name="fold_own",
    )(spot, kept, taken)


def update_kernel(rate, master, own, first, second, third, updated, short):
    grad = (own[...] + first[...].astype(jnp.float32)) + (
        second[...].astype(jnp.float32) + third[...].astype(jnp.float32)
    )
    new = master[...] - rate[0] * grad.T
    updated[...] = new
    short[...] = new.astype(jnp.bfloat16)


def update_of(rate, master, *parts):
    return pl.pallas_call(
        update_kernel,
        in_specs=[IN_SMEM] + [IN_VMEM] * 5,
        out_specs=[IN_VMEM] * 2,
        out_shape=[
            jax.ShapeDtypeStruct((ROWS, KW), jnp.float32),
            jax.ShapeDtypeStruct((ROWS, KW), jnp.bfloat16),
        ],
        compiler_params=PARAMS,
        cost_estimate=pl.CostEstimate(flops=8 * ROWS * KW, bytes_accessed=2 << 20, transcendentals=0),
        name="update",
    )(rate, master, *parts)


def mix_kernel(updated, other, mixed):
    mixed[...] = 0.5 * (updated[...] + other[...].astype(jnp.float32))


def mix_of(updated, other):
    return pl.pallas_call(
        mix_kernel,
        in_specs=[IN_VMEM] * 2,
        out_specs=IN_VMEM,
        out_shape=jax.ShapeDtypeStruct((ROWS, KW), jnp.float32),
        compiler_params=PARAMS,
        cost_estimate=pl.CostEstimate(flops=2 * ROWS * KW, bytes_accessed=2 << 20, transcendentals=0),
        name="mix",
    )(updated, other)


def keys_kernel(spot, inputs, cotan, mine, theirs, forward, backward, total):
    core, across = spot[0], spot[1]
    over_width = (((1,), (1,)), ((), ()))
    for y in range(RINGS):
        for side in range(SPAN):
            for rows, whose in ((mine, core), (theirs, 1 - core)):
                at = columns(SIDES * y + CORES * (across ^ side) + whose)
                part = rows[y, side]
                product = jnp.dot(inputs[:, at], part, preferred_element_type=jnp.float32)
                if y == 0 and side == 0 and rows is mine:
                    total[...] = product
                else:
                    total[...] += product
                back = lax.dot_general(cotan[...], part, over_width, preferred_element_type=jnp.float32)
                backward[:, at] = (back * SCALE).astype(jnp.bfloat16)
    forward[...] = (total[...] * SCALE).astype(jnp.bfloat16)


def keys_of(spot, inputs, cotan, mine, theirs):
    tokens = inputs.shape[0]
    return pl.pallas_call(
        keys_kernel,
        in_specs=[IN_SMEM] + [IN_VMEM] * 4,
        out_specs=[IN_VMEM] * 2,
        scratch_shapes=[pltpu.VMEM((tokens, KW), jnp.float32)],
        out_shape=[
            jax.ShapeDtypeStruct((tokens, KW), jnp.bfloat16),
            jax.ShapeDtypeStruct((tokens, D), jnp.bfloat16),
        ],
        compiler_params=PARAMS,
        cost_estimate=pl.CostEstimate(flops=tokens * D, bytes_accessed=1 << 20, transcendentals=0),
        name="keys_and_input_gradient",
    )(spot, inputs, cotan, mine, theirs)


def step(bit, inputs, master, cotan, rate):
    place = lax.axis_index("fsdp")
    spot = jnp.stack((place % CORES, place // CORES % SPAN, place // SIDES)).astype(jnp.int32)

    near_weights = swapped(master.astype(jnp.bfloat16), "fsdp", CORES)
    tokens = (inputs, swapped(inputs, "fsdp", 1), cotan, swapped(cotan, "fsdp", 1))
    kept, given = terms_of(spot, *tokens)
    taken = swapped(given, "fsdp", CORES)

    mine = along_y(copies_of(master, after(near_weights, given)))

    sent = fold_of(spot, kept, taken)
    own = own_of(spot, kept, after(taken, sent[0]))
    arrived = [shifted(part, hops) for hops, part in zip((1, 2, 3), sent)]
    theirs = swapped(after(mine, sent[0]), "fsdp", 1)
    updated, short = update_of(rate[None], master, own, *arrived)
    other = swapped(short, "rep", 1 << bit)
    projected, input_grad = keys_of(spot, inputs, cotan, mine, theirs)
    mixed = mix_of(updated, after(other, projected))
    return (projected[None], input_grad[None], mixed[None])


def body(activations, weights, cotangent, step_index):
    rate = 0.3 / jnp.sqrt(1.0 + step_index[0].astype(jnp.float32) / 50.0)
    branches = [partial(step, bit) for bit in range(BITS)]
    return lax.switch(step_index[0] % BITS, branches, activations[0], weights[0], cotangent[0], rate)


def solution(mesh):
    return jax.shard_map(
        body,
        mesh=mesh,
        in_specs=(P("rep", "fsdp", None), P("rep", "fsdp", None), P("rep", "fsdp", None), P()),
        out_specs=(P("rep", "fsdp", None), P("rep", "fsdp", None), P("rep", "fsdp", None)),
        check_vma=False,
    )
```

```python
from functools import partial

import jax
import jax.numpy as jnp
from jax import lax
from jax.experimental import pallas as pl
from jax.experimental.pallas import tpu as pltpu
from jax.sharding import PartitionSpec as P

D = 4096
KW = 512
BITS = 3
CORES = 2
SPAN = 2
RINGS = 4
SIDES = CORES * SPAN
ROWS = D // (SIDES * RINGS)
HALF = D // CORES
SCALE = D ** (-0.5)
ALONG_Y = [[side + SIDES * y for y in range(RINGS)] for side in range(SIDES)]
IN_VMEM = pl.BlockSpec(memory_space=pltpu.VMEM)
IN_SMEM = pl.BlockSpec(memory_space=pltpu.SMEM)
PARAMS = pltpu.CompilerParams(vmem_limit_bytes=16 << 20)
LIGHT = pl.CostEstimate(flops=1 << 20, bytes_accessed=1 << 20, transcendentals=0)
HEAVY = pl.CostEstimate(flops=1 << 38, bytes_accessed=1 << 20, transcendentals=0)


def shaped(*shape, dtype=jnp.bfloat16):
    return jax.ShapeDtypeStruct(shape, dtype)


def local(kernel, outs, cost, scalars, *operands, scratch=()):
    return pl.pallas_call(
        kernel,
        in_specs=[IN_SMEM] + [IN_VMEM] * len(operands),
        out_specs=[IN_VMEM] * len(outs),
        out_shape=list(outs),
        scratch_shapes=list(scratch),
        compiler_params=PARAMS,
        cost_estimate=cost,
        name=kernel.__name__,
    )(scalars, *operands)


def swapped(block, axis, apart):
    count = lax.axis_size(axis)
    return lax.ppermute(block, axis, [(low, low ^ apart) for low in range(count)])


def along_y(block):
    return lax.all_to_all(block, "fsdp", 0, 0, tiled=True, axis_index_groups=ALONG_Y)


def shifted(block, hops):
    count = SIDES * RINGS
    return lax.ppermute(block, "fsdp", [(place, (place + SIDES * hops) % count) for place in range(count)])


def after(value, earlier):
    return lax.optimization_barrier((value, earlier))[0]


def columns(block):
    return pl.ds(pl.multiple_of(block * ROWS, ROWS), ROWS)


def pack(spot, inputs, cotan, packed):
    for k in range(SPAN * RINGS):
        packed[:, k * ROWS : (k + 1) * ROWS] = inputs[:, columns(CORES * k + 1 - spot[0])]
    packed[:, HALF:] = cotan[...]


def gradient_terms(spot, inputs, cotan, partner, own, kept, far, last):
    turned = cotan[...].T
    partner_turned = partner[:, HALF:].T
    for side, outs in ((1 - spot[1], (last, far, far, last)), (spot[1], (own, kept, kept, kept))):
        for hops in (2, 1, 3, 0):
            k = SPAN * lax.rem(spot[2] + hops, RINGS) + side
            total = jnp.dot(turned, inputs[:, columns(CORES * k + spot[0])], preferred_element_type=jnp.float32)
            total += jnp.dot(partner_turned, partner[:, columns(k)], preferred_element_type=jnp.float32)
            if outs[hops] is own:
                own[...] = total * SCALE
            elif outs[hops] is last:
                last[0 if hops else 1] = (total * SCALE).astype(jnp.bfloat16)
            else:
                outs[hops][hops - 1] = (total * SCALE).astype(jnp.bfloat16)


def fold_far(_, kept, far, first, second):
    for at, out in enumerate((first, second)):
        out[...] = (kept[at].astype(jnp.float32) + far[at].astype(jnp.float32)).astype(jnp.bfloat16)


def fold_last(_, kept, last, third):
    third[...] = (kept[2].astype(jnp.float32) + last[0].astype(jnp.float32)).astype(jnp.bfloat16)


def fold_own(_, own, last, home):
    home[...] = own[...] + last[1].astype(jnp.float32)


def update(rate, master, home, first, second, third, updated, short):
    near = home[...] + first[...].astype(jnp.float32)
    grad = near + (second[...].astype(jnp.float32) + third[...].astype(jnp.float32))
    new = master[...] - rate[0] * grad.T
    updated[...] = new
    short[...] = new.astype(jnp.bfloat16)


def mix(_, updated, other, mixed):
    mixed[...] = 0.5 * (updated[...] + other[...].astype(jnp.float32))


def own_copies(_, master, half, out):
    half[...] = master[...].astype(jnp.bfloat16)
    for y in range(RINGS):
        out[y] = half[...]


def near_copies(_, near, out):
    for y in range(RINGS):
        out[y] = near[...]


def keys(spot, inputs, cotan, mine, mine_near, theirs, theirs_near, forward, backward, total):
    core, across = spot[0], spot[1]
    over_width = (((1,), (1,)), ((), ()))
    sources = ((mine, across, core), (mine_near, 1 - across, core))
    sources += ((theirs, across, 1 - core), (theirs_near, 1 - across, 1 - core))
    total[...] = jnp.zeros_like(total)
    for y in range(RINGS):
        for rows, side, whose in sources:
            at = columns(SIDES * y + CORES * side + whose)
            total[...] += jnp.dot(inputs[:, at], rows[y], preferred_element_type=jnp.float32)
            back = lax.dot_general(cotan[...], rows[y], over_width, preferred_element_type=jnp.float32)
            backward[:, at] = (back * SCALE).astype(jnp.bfloat16)
    forward[...] = (total[...] * SCALE).astype(jnp.bfloat16)


def step(bit, inputs, master, cotan, rate):
    place = lax.axis_index("fsdp")
    spot = jnp.stack((place % CORES, place // CORES % SPAN, place // SIDES)).astype(jnp.int32)
    tokens = inputs.shape[0]
    block, wide = shaped(KW, ROWS), shaped(KW, ROWS, dtype=jnp.float32)
    copies = shaped(RINGS, ROWS, KW)

    (packed,) = local(pack, [shaped(tokens, HALF + KW)], LIGHT, spot, inputs, cotan)
    partner = swapped(packed, "fsdp", 1)
    half_weights, copied = local(own_copies, [shaped(ROWS, KW), copies], LIGHT, spot, master)
    near_weights = swapped(half_weights, "fsdp", CORES)
    mine = along_y(copied)

    own, kept, far, last = local(
        gradient_terms,
        [wide, shaped(3, KW, ROWS), shaped(2, KW, ROWS), shaped(2, KW, ROWS)],
        LIGHT, spot, inputs, cotan, partner,
    )
    far = swapped(far, "fsdp", CORES)
    (copied,) = local(near_copies, [copies], pl.CostEstimate(flops=1 << 32, bytes_accessed=1 << 20, transcendentals=0), spot, after(near_weights, own))
    mine_near = along_y(copied)
    last = swapped(after(last, copied), "fsdp", CORES)
    theirs = swapped(after(mine, own), "fsdp", 1)

    first, second = local(fold_far, [block] * 2, HEAVY, spot, kept, far)
    (third,) = local(fold_last, [block], HEAVY, spot, kept, after(last, first))
    (home,) = local(fold_own, [wide], HEAVY, spot, own, after(last, third))
    theirs_near = swapped(after(mine_near, third), "fsdp", 1)
    arrived = [shifted(part, hops) for hops, part in enumerate((first, second, third), 1)]
    updated, short = local(
        update, [shaped(ROWS, KW, dtype=jnp.float32), shaped(ROWS, KW)], LIGHT, rate[None], master, home, *arrived
    )
    other = swapped(short, "rep", 1 << bit)
    projected, input_grad = local(
        keys,
        [shaped(tokens, KW), shaped(tokens, D)],
        LIGHT, spot, inputs, cotan, mine, mine_near, theirs, theirs_near,
        scratch=[pltpu.VMEM((tokens, KW), jnp.float32)],
    )
    (mixed,) = local(mix, [shaped(ROWS, KW, dtype=jnp.float32)], LIGHT, spot, updated, after(other, projected))
    return (projected[None], input_grad[None], mixed[None])


def body(activations, weights, cotangent, step_index):
    rate = 0.3 / jnp.sqrt(1.0 + step_index[0].astype(jnp.float32) / 50.0)
    branches = [partial(step, bit) for bit in range(BITS)]
    return lax.switch(step_index[0] % BITS, branches, activations[0], weights[0], cotangent[0], rate)


def solution(mesh):
    return jax.shard_map(
        body,
        mesh=mesh,
        in_specs=(P("rep", "fsdp", None), P("rep", "fsdp", None), P("rep", "fsdp", None), P()),
        out_specs=(P("rep", "fsdp", None), P("rep", "fsdp", None), P("rep", "fsdp", None)),
        check_vma=False,
    )
```

```python
from functools import partial

import jax
import jax.numpy as jnp
from jax import lax
from jax.experimental import pallas as pl
from jax.experimental.pallas import tpu as pltpu
from jax.sharding import PartitionSpec as P

D = 4096
KW = 512
BITS = 3
CORES = 2
SPAN = 2
RINGS = 4
SIDES = CORES * SPAN
ROWS = D // (SIDES * RINGS)
HALF = D // CORES
SCALE = D ** (-0.5)
ALONG_Y = [[side + SIDES * y for y in range(RINGS)] for side in range(SIDES)]
IN_VMEM = pl.BlockSpec(memory_space=pltpu.VMEM)
IN_SMEM = pl.BlockSpec(memory_space=pltpu.SMEM)
PARAMS = pltpu.CompilerParams(vmem_limit_bytes=16 << 20)
LIGHT = pl.CostEstimate(flops=1 << 20, bytes_accessed=1 << 20, transcendentals=0)
HEAVY = pl.CostEstimate(flops=1 << 38, bytes_accessed=1 << 32, transcendentals=0)
MEDIUM = pl.CostEstimate(flops=1 << 33, bytes_accessed=1 << 26, transcendentals=0)
FOLD = pl.CostEstimate(flops=1 << 38, bytes_accessed=1 << 20, transcendentals=0)


def shaped(*shape, dtype=jnp.bfloat16):
    return jax.ShapeDtypeStruct(shape, dtype)


def close(*shape, dtype=jnp.bfloat16):
    return pltpu.VMEM(shape, dtype)


def held(block):
    return pltpu.with_memory_space_constraint(block, pltpu.VMEM)


def local(kernel, outs, cost, scalars, *operands, scratch=()):
    return pl.pallas_call(
        kernel,
        in_specs=[IN_SMEM] + [IN_VMEM] * len(operands),
        out_specs=[IN_VMEM] * len(outs),
        out_shape=list(outs),
        scratch_shapes=list(scratch),
        compiler_params=PARAMS,
        cost_estimate=cost,
        name=kernel.__name__,
    )(scalars, *operands)


def swapped(block, axis, apart):
    count = lax.axis_size(axis)
    return lax.ppermute(block, axis, [(low, low ^ apart) for low in range(count)])


def along_y(block):
    return lax.all_to_all(block, "fsdp", 0, 0, tiled=True, axis_index_groups=ALONG_Y)


def shifted(block, hops):
    count = SIDES * RINGS
    return lax.ppermute(block, "fsdp", [(place, (place + SIDES * hops) % count) for place in range(count)])


def after(value, earlier):
    return lax.optimization_barrier((value, earlier))[0]


def columns(block):
    return pl.ds(pl.multiple_of(block * ROWS, ROWS), ROWS)


def pack(spot, inputs, cotan, packed):
    for k in range(SPAN * RINGS):
        packed[:, k * ROWS : (k + 1) * ROWS] = inputs[:, columns(CORES * k + 1 - spot[0])]
    packed[:, HALF:] = cotan[...]


def gradient_terms(spot, inputs, cotan, partner, kept, given):
    turned = cotan[...].T
    partner_turned = partner[:, HALF:].T
    for out, side in ((given, 1 - spot[1]), (kept, spot[1])):
        for y in range(RINGS):
            k = SPAN * y + side
            total = jnp.dot(turned, inputs[:, columns(CORES * k + spot[0])], preferred_element_type=jnp.float32)
            total += jnp.dot(partner_turned, partner[:, columns(k)], preferred_element_type=jnp.float32)
            out[y] = (total * SCALE).astype(jnp.bfloat16)


def fold(_, kept, taken, both):
    for y in range(RINGS):
        both[y] = (kept[y].astype(jnp.float32) + taken[y].astype(jnp.float32)).astype(jnp.bfloat16)


def update(rate, master, terms, updated, short):
    parts = [terms[y].astype(jnp.float32) for y in range(RINGS)]
    grad = (parts[0] + parts[1]) + (parts[2] + parts[3])
    new = master[...] - rate[0] * grad.T
    updated[...] = new
    short[...] = new.astype(jnp.bfloat16)


def mix(_, updated, other, mixed):
    mixed[...] = 0.5 * (updated[...] + other[...].astype(jnp.float32))


def pair_up(_, half, near, pair):
    pair[0] = half[...]
    pair[1] = near[...]


def gather(_, *refs):
    for hops, piece in enumerate(refs[:-1]):
        refs[-1][hops] = piece[...]


def keys(spot, inputs, cotan, mine, theirs, forward, backward, total):
    over_width = (((1,), (1,)), ((), ()))
    total[...] = jnp.zeros_like(total)
    for hops in range(RINGS):
        y = lax.rem(spot[2] + RINGS - hops, RINGS)
        for side in range(SPAN):
            for rows, core in ((mine, spot[0]), (theirs, 1 - spot[0])):
                at = columns(SIDES * y + CORES * (spot[1] ^ side) + core)
                part = rows[hops, side]
                total[...] += jnp.dot(inputs[:, at], part, preferred_element_type=jnp.float32)
                back = lax.dot_general(cotan[...], part, over_width, preferred_element_type=jnp.float32)
                backward[:, at] = (back * SCALE).astype(jnp.bfloat16)
    forward[...] = (total[...] * SCALE).astype(jnp.bfloat16)


def step(bit, inputs, master, cotan, rate):
    place = lax.axis_index("fsdp")
    spot = jnp.stack((place % CORES, place // CORES % SPAN, place // SIDES)).astype(jnp.int32)
    tokens = inputs.shape[0]
    block, wide = close(KW, ROWS), close(KW, ROWS, dtype=jnp.float32)

    (packed,) = local(pack, [close(tokens, HALF + KW)], LIGHT, spot, inputs, cotan)
    partner = swapped(packed, "fsdp", 1)
    half_weights = master.astype(jnp.bfloat16)
    near_weights = swapped(half_weights, "fsdp", CORES)

    kept, given = local(
        gradient_terms, [close(RINGS, KW, ROWS)] * 2, LIGHT, spot, inputs, cotan, held(partner)
    )
    taken = swapped(given, "fsdp", CORES)
    (pair,) = local(pair_up, [close(SPAN, ROWS, KW)], MEDIUM, spot, half_weights, held(after(near_weights, kept)))
    pieces = [shifted(pair, hops) for hops in (1, 2, 3)]

    (both,) = local(fold, [close(RINGS, KW, ROWS)], FOLD, spot, kept, held(taken))
    terms = along_y(both)
    (mine,) = local(gather, [close(RINGS, SPAN, ROWS, KW)], MEDIUM, spot, pair, *map(held, [after(piece, both) for piece in pieces]))
    theirs = swapped(mine, "fsdp", 1)
    updated, short = local(
        update, [close(ROWS, KW, dtype=jnp.float32), close(ROWS, KW)], HEAVY, rate[None], master, held(terms)
    )
    other = swapped(short, "rep", 1 << bit)
    projected, input_grad = local(
        keys,
        [shaped(tokens, KW), shaped(tokens, D)],
        LIGHT, spot, inputs, cotan, held(mine), held(theirs),
        scratch=[pltpu.VMEM((tokens, KW), jnp.float32)],
    )
    (mixed,) = local(mix, [shaped(ROWS, KW, dtype=jnp.float32)], LIGHT, spot, updated, held(after(other, projected)))
    return (projected[None], input_grad[None], mixed[None])


def body(activations, weights, cotangent, step_index):
    rate = 0.3 / jnp.sqrt(1.0 + step_index[0].astype(jnp.float32) / 50.0)
    branches = [partial(step, bit) for bit in range(BITS)]
    return lax.switch(step_index[0] % BITS, branches, activations[0], weights[0], cotangent[0], rate)


def solution(mesh):
    return jax.shard_map(
        body,
        mesh=mesh,
        in_specs=(P("rep", "fsdp", None), P("rep", "fsdp", None), P("rep", "fsdp", None), P()),
        out_specs=(P("rep", "fsdp", None), P("rep", "fsdp", None), P("rep", "fsdp", None)),
        check_vma=False,
    )
```

```python
from functools import partial

import jax
import jax.numpy as jnp
from jax import lax
from jax.experimental import pallas as pl
from jax.experimental.pallas import tpu as pltpu
from jax.sharding import PartitionSpec as P

D = 4096
KW = 512
BITS = 3
CORES = 2
SPAN = 2
RINGS = 4
SIDES = CORES * SPAN
ROWS = D // (SIDES * RINGS)
HALF = D // CORES
SCALE = D ** (-0.5)
ALONG_Y = [[side + SIDES * y for y in range(RINGS)] for side in range(SIDES)]
IN_VMEM = pl.BlockSpec(memory_space=pltpu.VMEM)
IN_SMEM = pl.BlockSpec(memory_space=pltpu.SMEM)
PARAMS = pltpu.CompilerParams(vmem_limit_bytes=16 << 20)
LIGHT = pl.CostEstimate(flops=1 << 20, bytes_accessed=1 << 20, transcendentals=0)
HEAVY = pl.CostEstimate(flops=1 << 38, bytes_accessed=1 << 32, transcendentals=0)
MEDIUM = pl.CostEstimate(flops=1 << 33, bytes_accessed=1 << 26, transcendentals=0)
FOLD = pl.CostEstimate(flops=1 << 38, bytes_accessed=1 << 20, transcendentals=0)


def shaped(*shape, dtype=jnp.bfloat16):
    return jax.ShapeDtypeStruct(shape, dtype)


def close(*shape, dtype=jnp.bfloat16):
    return pltpu.VMEM(shape, dtype)


def held(block):
    return pltpu.with_memory_space_constraint(block, pltpu.VMEM)


def local(kernel, outs, cost, scalars, *operands, scratch=()):
    return pl.pallas_call(
        kernel,
        in_specs=([] if scalars is None else [IN_SMEM]) + [IN_VMEM] * len(operands),
        out_specs=[IN_VMEM] * len(outs),
        out_shape=list(outs),
        scratch_shapes=list(scratch),
        compiler_params=PARAMS,
        cost_estimate=cost,
        name=kernel.__name__,
    )(*([] if scalars is None else [scalars]), *operands)


def swapped(block, axis, apart):
    count = lax.axis_size(axis)
    return lax.ppermute(block, axis, [(low, low ^ apart) for low in range(count)])


def along_y(block):
    return lax.all_to_all(block, "fsdp", 0, 0, tiled=True, axis_index_groups=ALONG_Y)


def shifted(block, hops):
    count = SIDES * RINGS
    return lax.ppermute(block, "fsdp", [(place, (place + SIDES * hops) % count) for place in range(count)])


def after(value, earlier):
    return lax.optimization_barrier((value, earlier))[0]


def columns(block):
    return pl.ds(pl.multiple_of(block * ROWS, ROWS), ROWS)


def pack(spot, inputs, cotan, packed):
    for k in range(SPAN * RINGS):
        packed[:, k * ROWS : (k + 1) * ROWS] = inputs[:, columns(CORES * k + 1 - spot[0])]
    packed[:, HALF:] = cotan[...]


def gradient_terms(spot, inputs, cotan, partner, kept, given):
    turned = cotan[...].T
    partner_turned = partner[:, HALF:].T
    for out, side in ((given, 1 - spot[1]), (kept, spot[1])):
        for y in range(RINGS):
            k = SPAN * y + side
            total = jnp.dot(turned, inputs[:, columns(CORES * k + spot[0])], preferred_element_type=jnp.float32)
            total += jnp.dot(partner_turned, partner[:, columns(k)], preferred_element_type=jnp.float32)
            out[y] = (total * SCALE).astype(jnp.bfloat16)


def fold(kept, taken, both):
    for y in range(RINGS):
        both[y] = (kept[y].astype(jnp.float32) + taken[y].astype(jnp.float32)).astype(jnp.bfloat16)


def update(rate, master, terms, updated, short):
    parts = [terms[y].astype(jnp.float32) for y in range(RINGS)]
    grad = (parts[0] + parts[1]) + (parts[2] + parts[3])
    new = master[...] - rate[0] * grad.T
    updated[...] = new
    short[...] = new.astype(jnp.bfloat16)


def mix(updated, other, mixed):
    mixed[...] = 0.5 * (updated[...] + other[...].astype(jnp.float32))


def pair_up(half, near, pair):
    pair[0] = half[...]
    pair[1] = near[...]


def gather(*refs):
    for hops, piece in enumerate(refs[:-1]):
        refs[-1][hops] = piece[...]


def keys(spot, inputs, cotan, mine, theirs, forward, backward, total):
    over_width = (((1,), (1,)), ((), ()))
    total[...] = jnp.zeros_like(total)
    for hops in range(RINGS):
        y = lax.rem(spot[2] + RINGS - hops, RINGS)
        for side in range(SPAN):
            for rows, core in ((mine, spot[0]), (theirs, 1 - spot[0])):
                at = columns(SIDES * y + CORES * (spot[1] ^ side) + core)
                part = rows[hops, side]
                total[...] += jnp.dot(inputs[:, at], part, preferred_element_type=jnp.float32)
                back = lax.dot_general(cotan[...], part, over_width, preferred_element_type=jnp.float32)
                backward[:, at] = (back * SCALE).astype(jnp.bfloat16)
    forward[...] = (total[...] * SCALE).astype(jnp.bfloat16)


def step(bit, inputs, master, cotan, rate):
    place = lax.axis_index("fsdp")
    spot = jnp.stack((place % CORES, place // CORES % SPAN, place // SIDES)).astype(jnp.int32)
    tokens = inputs.shape[0]
    block, wide = close(KW, ROWS), close(KW, ROWS, dtype=jnp.float32)

    (packed,) = local(pack, [close(tokens, HALF + KW)], LIGHT, spot, inputs, cotan)
    partner = swapped(packed, "fsdp", 1)
    half_weights = master.astype(jnp.bfloat16)
    near_weights = swapped(half_weights, "fsdp", CORES)

    kept, given = local(
        gradient_terms, [close(RINGS, KW, ROWS)] * 2, LIGHT, spot, inputs, cotan, held(partner)
    )
    taken = swapped(given, "fsdp", CORES)
    (pair,) = local(pair_up, [close(SPAN, ROWS, KW)], MEDIUM, None, half_weights, held(after(near_weights, kept)))
    pieces = [shifted(pair, hops) for hops in (1, 2, 3)]

    (both,) = local(fold, [close(RINGS, KW, ROWS)], FOLD, None, kept, held(taken))
    terms = along_y(both)
    (mine,) = local(gather, [close(RINGS, SPAN, ROWS, KW)], MEDIUM, None, pair, *map(held, [after(piece, both) for piece in pieces]))
    theirs = swapped(mine, "fsdp", 1)
    updated, short = local(
        update, [close(ROWS, KW, dtype=jnp.float32), close(ROWS, KW)], HEAVY, rate[None], master, held(terms)
    )
    other = swapped(short, "rep", 1 << bit)
    projected, input_grad = local(
        keys,
        [shaped(tokens, KW), shaped(tokens, D)],
        LIGHT, spot, inputs, cotan, held(mine), held(theirs),
        scratch=[pltpu.VMEM((tokens, KW), jnp.float32)],
    )
    (mixed,) = local(mix, [shaped(ROWS, KW, dtype=jnp.float32)], LIGHT, None, updated, held(after(other, projected)))
    return (projected[None], input_grad[None], mixed[None])


def body(activations, weights, cotangent, step_index):
    rate = 0.3 / jnp.sqrt(1.0 + step_index[0].astype(jnp.float32) / 50.0)
    branches = [partial(step, bit) for bit in range(BITS)]
    return lax.switch(step_index[0] % BITS, branches, activations[0], weights[0], cotangent[0], rate)


def solution(mesh):
    return jax.shard_map(
        body,
        mesh=mesh,
        in_specs=(P("rep", "fsdp", None), P("rep", "fsdp", None), P("rep", "fsdp", None), P()),
        out_specs=(P("rep", "fsdp", None), P("rep", "fsdp", None), P("rep", "fsdp", None)),
        check_vma=False,
    )
```

```python
from functools import partial

import jax
import jax.numpy as jnp
from jax import lax
from jax.experimental import pallas as pl
from jax.experimental.pallas import tpu as pltpu
from jax.sharding import PartitionSpec as P

D = 4096
KW = 512
BITS = 3
CORES = 2
SPAN = 2
RINGS = 4
SIDES = CORES * SPAN
ROWS = D // (SIDES * RINGS)
HALF = D // CORES
SCALE = D ** (-0.5)
ALONG_Y = [[side + SIDES * y for y in range(RINGS)] for side in range(SIDES)]
IN_VMEM = pl.BlockSpec(memory_space=pltpu.VMEM)
IN_SMEM = pl.BlockSpec(memory_space=pltpu.SMEM)
PARAMS = pltpu.CompilerParams(vmem_limit_bytes=16 << 20)
LIGHT = pl.CostEstimate(flops=1 << 20, bytes_accessed=1 << 20, transcendentals=0)
HEAVY = pl.CostEstimate(flops=1 << 38, bytes_accessed=1 << 32, transcendentals=0)
MEDIUM = pl.CostEstimate(flops=1 << 33, bytes_accessed=1 << 26, transcendentals=0)
FOLD = pl.CostEstimate(flops=1 << 38, bytes_accessed=1 << 20, transcendentals=0)


def shaped(*shape, dtype=jnp.bfloat16):
    return jax.ShapeDtypeStruct(shape, dtype)


def close(*shape, dtype=jnp.bfloat16):
    return pltpu.VMEM(shape, dtype)


def held(block):
    return pltpu.with_memory_space_constraint(block, pltpu.VMEM)


def local(kernel, outs, cost, scalars, *operands, scratch=()):
    return pl.pallas_call(
        kernel,
        in_specs=([] if scalars is None else [IN_SMEM]) + [IN_VMEM] * len(operands),
        out_specs=[IN_VMEM] * len(outs),
        out_shape=list(outs),
        scratch_shapes=list(scratch),
        compiler_params=PARAMS,
        cost_estimate=cost,
        name=kernel.__name__,
    )(*([] if scalars is None else [scalars]), *operands)


def swapped(block, axis, apart):
    count = lax.axis_size(axis)
    return lax.ppermute(block, axis, [(low, low ^ apart) for low in range(count)])


def along_y(block):
    return lax.all_to_all(block, "fsdp", 0, 0, tiled=True, axis_index_groups=ALONG_Y)


def shifted(block, hops):
    count = SIDES * RINGS
    return lax.ppermute(block, "fsdp", [(place, (place + SIDES * hops) % count) for place in range(count)])


def after(value, earlier):
    return lax.optimization_barrier((value, earlier))[0]


def position():
    place = lax.axis_index("fsdp")
    return place % CORES, place // CORES % SPAN, place // SIDES


def columns(block):
    return pl.ds(pl.multiple_of(block * ROWS, ROWS), ROWS)


def pack(inputs, cotan, packed):
    spot = position()
    for k in range(SPAN * RINGS):
        packed[:, k * ROWS : (k + 1) * ROWS] = inputs[:, columns(CORES * k + 1 - spot[0])]
    packed[:, HALF:] = cotan[...]


def gradient_terms(inputs, cotan, partner, kept, given):
    spot = position()
    turned = cotan[...].T
    partner_turned = partner[:, HALF:].T
    for out, side in ((given, 1 - spot[1]), (kept, spot[1])):
        for y in range(RINGS):
            k = SPAN * y + side
            total = jnp.dot(turned, inputs[:, columns(CORES * k + spot[0])], preferred_element_type=jnp.float32)
            total += jnp.dot(partner_turned, partner[:, columns(k)], preferred_element_type=jnp.float32)
            out[y] = (total * SCALE).astype(jnp.bfloat16)


def fold(kept, taken, both):
    for y in range(RINGS):
        both[y] = (kept[y].astype(jnp.float32) + taken[y].astype(jnp.float32)).astype(jnp.bfloat16)


def update(rate, master, terms, updated, short):
    parts = [terms[y].astype(jnp.float32) for y in range(RINGS)]
    grad = (parts[0] + parts[1]) + (parts[2] + parts[3])
    new = master[...] - rate[0] * grad.T
    updated[...] = new
    short[...] = new.astype(jnp.bfloat16)


def mix(updated, other, mixed):
    mixed[...] = 0.5 * (updated[...] + other[...].astype(jnp.float32))


def pair_up(half, near, pair):
    pair[0] = half[...]
    pair[1] = near[...]


def gather(*refs):
    for hops, piece in zip((0, 1, 3, 2), refs[:-1]):
        refs[-1][hops] = piece[...]


def keys(inputs, cotan, mine, theirs, forward, backward, total):
    spot = position()
    over_width = (((1,), (1,)), ((), ()))
    total[...] = jnp.zeros_like(total)
    for hops in range(RINGS):
        y = lax.rem(spot[2] + RINGS - hops, RINGS)
        for side in range(SPAN):
            for rows, core in ((mine, spot[0]), (theirs, 1 - spot[0])):
                at = columns(SIDES * y + CORES * (spot[1] ^ side) + core)
                part = rows[hops, side]
                total[...] += jnp.dot(inputs[:, at], part, preferred_element_type=jnp.float32)
                back = lax.dot_general(cotan[...], part, over_width, preferred_element_type=jnp.float32)
                backward[:, at] = (back * SCALE).astype(jnp.bfloat16)
    forward[...] = (total[...] * SCALE).astype(jnp.bfloat16)


def step(bit, inputs, master, cotan, rate):
    tokens = inputs.shape[0]
    block, wide = close(KW, ROWS), close(KW, ROWS, dtype=jnp.float32)

    (packed,) = local(pack, [close(tokens, HALF + KW)], LIGHT, None, inputs, cotan)
    partner = swapped(packed, "fsdp", 1)
    half_weights = master.astype(jnp.bfloat16)
    near_weights = swapped(half_weights, "fsdp", CORES)

    kept, given = local(
        gradient_terms, [close(RINGS, KW, ROWS)] * 2, LIGHT, None, inputs, cotan, held(partner)
    )
    taken = swapped(given, "fsdp", CORES)
    (pair,) = local(pair_up, [close(SPAN, ROWS, KW)], MEDIUM, None, half_weights, held(after(near_weights, kept)))
    pieces = [shifted(pair, hops) for hops in (1, 3, 2)]

    (both,) = local(fold, [close(RINGS, KW, ROWS)], FOLD, None, kept, held(taken))
    terms = along_y(both)
    (mine,) = local(gather, [close(RINGS, SPAN, ROWS, KW)], MEDIUM, None, pair, *map(held, [after(piece, both) for piece in pieces]))
    theirs = swapped(mine, "fsdp", 1)
    updated, short = local(
        update, [close(ROWS, KW, dtype=jnp.float32), close(ROWS, KW)], HEAVY, rate[None], master, held(terms)
    )
    other = swapped(short, "rep", 1 << bit)
    projected, input_grad = local(
        keys,
        [shaped(tokens, KW), shaped(tokens, D)],
        LIGHT, None, inputs, cotan, held(mine), held(theirs),
        scratch=[pltpu.VMEM((tokens, KW), jnp.float32)],
    )
    (mixed,) = local(mix, [shaped(ROWS, KW, dtype=jnp.float32)], LIGHT, None, updated, held(after(other, projected)))
    return (projected[None], input_grad[None], mixed[None])


def body(activations, weights, cotangent, step_index):
    rate = 0.3 / jnp.sqrt(1.0 + step_index[0].astype(jnp.float32) / 50.0)
    branches = [partial(step, bit) for bit in range(BITS)]
    return lax.switch(step_index[0] % BITS, branches, activations[0], weights[0], cotangent[0], rate)


def solution(mesh):
    return jax.shard_map(
        body,
        mesh=mesh,
        in_specs=(P("rep", "fsdp", None), P("rep", "fsdp", None), P("rep", "fsdp", None), P()),
        out_specs=(P("rep", "fsdp", None), P("rep", "fsdp", None), P("rep", "fsdp", None)),
        check_vma=False,
    )
```
